1024 devices in a mesh: runs: 64 (over z_lo, x), feat: 16 (over y, z_hi, core).
Axes of the slice: x: 4, y: 4, z: 32 (z_hi: 2, z_lo: 16; z = z_hi * 16 + z_lo), core: 2. Of those that a mesh axis runs over, the one named last changes fastest.
Arguments:
- samples: bfloat16 [2560, 24576], P('runs', 'feat'), may hold values from -12 to 12, as said below
Outputs:
- markov: float32 [2560, 2560], P('runs', 'feat')
The draws below stay inside these ranges and needn't reach their ends.
Inputs may be any that keep to these rules, and one draw needn't show every extreme that they name: `samples`: real-valued deformation features.
All inputs are finite; a program needn't handle non-finite values.
Results may differ from the reference program's by a relative error of at most 0.0003.
Values may be sent and summed in bfloat16 or wider, within the bound.
A program may use at most 32 MiB of HBM per device.

```python
import jax
import jax.numpy as jnp

FEATURES = 24576
RUNS = 2560


def draw_samples(key, part):
    key = jax.random.fold_in(key, 11)
    key_scale, key_noise, key_coef, key_mode = jax.random.split(key, 4)
    scales = jnp.exp(jax.random.uniform(key_scale, (RUNS,), jnp.float32, jnp.log(0.4), jnp.log(1.6)))
    noise = jnp.clip(jax.random.normal(key_noise, (RUNS, FEATURES), jnp.float32), -4.0, 4.0)
    coefs = jnp.clip(jax.random.normal(key_coef, (RUNS, 4), jnp.float32), -3.0, 3.0) * 0.7
    modes = jnp.clip(jax.random.normal(key_mode, (4, FEATURES), jnp.float32), -3.0, 3.0)
    mixed = coefs[:, 0:1] * modes[0:1, :] + coefs[:, 1:2] * modes[1:2, :]
    mixed = mixed + coefs[:, 2:3] * modes[2:3, :] + coefs[:, 3:4] * modes[3:4, :]
    values = scales[:, None] * (noise + mixed)
    return jnp.clip(values, -12.0, 12.0).astype(jnp.bfloat16)


def setup_inputs(seed: int = 0) -> dict:
    keys = jax.random.split(jax.random.key(seed), 2)
    samples = draw_samples(jax.random.fold_in(keys[1], 71), 0)
    return {"samples": samples}


def reference(samples):
    gram = jnp.dot(samples, samples.T, preferred_element_type=jnp.float32)
    wide = samples.astype(jnp.float32)
    norms = jnp.sum(wide * wide, axis=1)
    dist = norms[:, None] + norms[None, :] - 2.0 * gram
    kernel = jnp.exp(-dist / (4.0 * FEATURES))
    density = jnp.sum(kernel, axis=1)
    scaled = kernel / (density[:, None] * density[None, :])
    degree = jnp.sum(scaled, axis=1)
    return (RUNS * 1.0) * scaled / degree[:, None]
```

```python
import functools

import jax
import jax.numpy as jnp
from jax import lax
from jax.experimental import pallas as pl
from jax.experimental.pallas import tpu as pltpu
from jax.sharding import PartitionSpec as P

MESH = pl.DeviceIdType.MESH
F32 = jnp.float32
NT = (((1,), (1,)), ((), ()))


def device(x, z, y, h, c):
    return (z * 4 + x, (y * 2 + h) * 2 + c)


def kernel(
    total, scale, s_ref, o_ref, abuf, bbuf, acat, bcat, tbuf, r1buf, swsend, owsend, swbuf, owbuf, d1buf, d2buf, gbuf,
    a_ss, a_rs, x_ss, x_rs, b_ss, b_rs, r1_ss, r1_rs, sw_ss, sw_rs, ow_ss, ow_rs, d1_ss, d1_rs, d2_ss, d2_rs, g_ss, g_rs,
):
    run, feat = lax.axis_index("runs"), lax.axis_index("feat")
    x, z = run % 4, run // 4
    u, v = z // 4, z % 4
    y, h, c = feat // 4, (feat // 2) % 2, feat % 2

    def copy(src, dst, ss, rs, to):
        return pltpu.make_async_remote_copy(
            src_ref=src, dst_ref=dst, send_sem=ss, recv_sem=rs, device_id=to, device_id_type=MESH
        )

    def is_me(to):
        return jnp.logical_and(to[0] == run, to[1] == feat)

    here = (run, feat)
    fv = 2 * h + c
    swap_c = jnp.where(u <= y, 0, 1)
    own_c = jnp.where(y < u, 0, 1)
    swap_from = [device(x, y * 4 + v, fv, hh, swap_c) for hh in range(2)]
    own_from = [[device(xx, u * 4 + fv, v, hh, own_c) for xx in range(4)] for hh in range(2)]
    swap_ok = [jnp.where(c == 0, u2 <= u, u2 > u) for u2 in range(4)]
    own_ok = [jnp.where(c == 0, u2 < u, u2 >= u) for u2 in range(4)]
    tile_ok = [jnp.where(c == 0, u2 <= u, u2 >= u) for u2 in range(4)]
    swap_to = [device(x, u2 * 4 + v, u, y // 2, y % 2) for u2 in range(4)]
    own_to = [[device(xx, u * 4 + y, u2, v // 2, v % 2) for xx in range(4)] for u2 in range(4)]

    near = [((x + dx) % 4, (v + dv) % 4) for dv in range(4) for dx in range(4) if (dx, dv) != (0, 0)]
    near_dev = [device(xx, u * 4 + vv, y, h, c) for xx, vv in near]
    us = [(u + d) % 4 for d in range(1, 4)]
    u_dev = [device(x, uu * 4 + v, y, h, c) for uu in us]
    fs = [(feat + d) % 16 for d in range(1, 16)]

    barrier = pltpu.get_barrier_semaphore()
    for to in near_dev + u_dev + [(run, ff) for ff in fs]:
        pl.semaphore_signal(barrier, inc=1, device_id=to, device_id_type=MESH)
    mine = 0
    for to in swap_from + own_from[0] + own_from[1]:
        same = is_me(to)
        mine = mine + jnp.where(same, 1, 0)

        @pl.when(jnp.logical_not(same))
        def _():
            pl.semaphore_signal(barrier, inc=1, device_id=to, device_id_type=MESH)

    pl.semaphore_wait(barrier, 33 + jnp.where(c == 0, 5 * u + 1, 19 - 5 * u) - mine)

    def b_out(i):
        return copy(s_ref, bbuf.at[u], b_ss.at[i], b_rs.at[u], u_dev[i])

    def b_sends(i):
        return jnp.where(c == 0, us[i] > u, us[i] < u)

    def a_out(d):
        return copy(s_ref, abuf.at[v, x], a_ss.at[d], a_rs.at[v], device(x, u * 4 + (v + d) % 4, y, h, c))

    def x_out(d, e):
        vv = (v + d) % 4
        src = s_ref if d == 0 else abuf.at[vv, x]
        return copy(src, abuf.at[vv, x], x_ss.at[d, e], x_rs.at[vv, x], device((x + e) % 4, z, y, h, c))

    for d in (1, 3, 2):
        a_out(d).start()
    for i in range(3):
        pl.when(b_sends(i))(b_out(i).start)
    for e in (1, 3, 2):
        x_out(0, e).start()
    abuf[v, x] = s_ref[...]
    bbuf[u] = s_ref[...]
    for d in (1, 3, 2):
        vv = (v + d) % 4
        copy(s_ref, abuf.at[vv, x], a_ss.at[d], a_rs.at[vv], here).wait_recv()
        for e in (1, 3, 2):
            x_out(d, e).start()
    for d in (0, 1, 3, 2):
        vv = (v + d) % 4
        for e in range(1, 4):
            xx = (x + e) % 4
            copy(s_ref, abuf.at[vv, xx], x_ss.at[d, e], x_rs.at[vv, xx], here).wait_recv()

    ones = jnp.ones((8, s_ref.shape[1]), jnp.bfloat16)
    norms = []
    for vv in range(4):
        wide = jnp.concatenate([abuf[vv, xx].astype(F32) for xx in range(4)], axis=0)
        acat[vv] = wide.astype(jnp.bfloat16)
        square = wide * wide
        high = square.astype(jnp.bfloat16)
        low = (square - high.astype(F32)).astype(jnp.bfloat16)
        norm = lax.dot_general(ones, high, NT, preferred_element_type=F32)
        norm = norm + lax.dot_general(ones, low, NT, preferred_element_type=F32)
        norms.append(norm[0:1])

    for i in range(3):
        uu = us[i]

        @pl.when(jnp.where(c == 0, uu < u, uu > u))
        def _():
            copy(s_ref, bbuf.at[uu], b_ss.at[i], b_rs.at[uu], here).wait_recv()

        @pl.when(jnp.where(c == 0, uu > u, uu < u))
        def _():
            bbuf[uu] = s_ref[...]

    wide = jnp.concatenate([bbuf[uu].astype(F32) for uu in range(4)], axis=0)
    bcat[...] = wide.astype(jnp.bfloat16)
    rownorm = jnp.sum(wide * wide, axis=1, keepdims=True)

    def r1_out(vv, u2):
        return copy(tbuf.at[vv, u2], r1buf.at[y, u2], r1_ss.at[vv, u2], r1_rs.at[y, u2], device(x, z, vv, h, c))

    for vv in range(4):
        gram = lax.dot_general(bcat[...], acat[vv], NT, preferred_element_type=F32)
        part = rownorm + norms[vv] - 2.0 * gram
        for u2 in range(4):
            tbuf[vv, u2] = part[u2 * 40 : u2 * 40 + 40]

        @pl.when(vv != y)
        def _():
            for u2 in range(4):
                pl.when(tile_ok[u2])(r1_out(vv, u2).start)

    for d in range(1, 4):
        yy = (y + d) % 4
        for u2 in range(4):

            @pl.when(tile_ok[u2])
            def _():
                copy(tbuf.at[0, u2], r1buf.at[yy, u2], r1_ss.at[0, u2], r1_rs.at[yy, u2], here).wait_recv()

    def sw_out(u2):
        return copy(swsend.at[u2], swbuf.at[h], sw_ss.at[u2], sw_rs.at[h], swap_to[u2])

    def ow_out(u2, xx):
        return copy(owsend.at[u2, xx], owbuf.at[h, x], ow_ss.at[u2, xx], ow_rs.at[h, x], own_to[u2][xx])

    for u2 in range(4):

        @pl.when(tile_ok[u2])
        def _():
            tile = tbuf[y, u2]
            for d in range(1, 4):
                tile = tile + r1buf[(y + d) % 4, u2]
            swsend[u2] = tile
            turned = tile.T
            for xx in range(4):
                owsend[u2, xx] = turned[xx * 40 : xx * 40 + 40]

        same = is_me(swap_to[u2])

        @pl.when(jnp.logical_and(swap_ok[u2], same))
        def _():
            swbuf[h] = swsend[u2]

        pl.when(jnp.logical_and(swap_ok[u2], jnp.logical_not(same)))(sw_out(u2).start)
        for xx in range(4):
            same = is_me(own_to[u2][xx])

            @pl.when(jnp.logical_and(own_ok[u2], same))
            def _():
                owbuf[h, x] = owsend[u2, xx]

            pl.when(jnp.logical_and(own_ok[u2], jnp.logical_not(same)))(ow_out(u2, xx).start)

    for hh in range(2):

        @pl.when(jnp.logical_not(is_me(swap_from[hh])))
        def _():
            copy(swsend.at[0], swbuf.at[hh], sw_ss.at[0], sw_rs.at[hh], here).wait_recv()

        for xx in range(4):

            @pl.when(jnp.logical_not(is_me(own_from[hh][xx])))
            def _():
                copy(owsend.at[0, 0], owbuf.at[hh, xx], ow_ss.at[0, 0], ow_rs.at[hh, xx], here).wait_recv()

    own = jnp.concatenate([owbuf[0, xx] + owbuf[1, xx] for xx in range(4)], axis=1)
    dist = swbuf[0] + swbuf[1] + own
    value = jnp.exp(-dist / scale)

    def d1_out(i):
        return copy(d1buf.at[v, x], d1buf.at[v, x], d1_ss.at[i], d1_rs.at[v, x], near_dev[i])

    d1buf[v, x] = jnp.sum(value, axis=0, keepdims=True)
    for i in range(15):
        d1_out(i).start()
    for xx, vv in near:
        copy(d1buf.at[v, x], d1buf.at[vv, xx], d1_ss.at[0], d1_rs.at[vv, xx], here).wait_recv()
    density = d1buf[0, 0]
    for i in range(1, 16):
        density = density + d1buf[i // 4, i % 4]

    def d2_out(i):
        return copy(d2buf.at[u], d2buf.at[u], d2_ss.at[i], d2_rs.at[u], u_dev[i])

    d2buf[u] = density
    for i in range(3):
        d2_out(i).start()
    for uu in us:
        copy(d2buf.at[u], d2buf.at[uu], d2_ss.at[0], d2_rs.at[uu], here).wait_recv()
    density = d2buf[0] + d2buf[1] + d2buf[2] + d2buf[3]

    scaled = value / density
    degree = jnp.sum(scaled, axis=1, keepdims=True)

    def g_out(i):
        return copy(gbuf.at[feat], gbuf.at[feat], g_ss.at[i], g_rs.at[feat], (run, fs[i]))

    gbuf[feat] = jnp.broadcast_to(degree, (40, 128)).T[0:1]
    for i in range(15):
        g_out(i).start()
    for ff in fs:
        copy(gbuf.at[feat], gbuf.at[ff], g_ss.at[0], g_rs.at[ff], here).wait_recv()
    degree = gbuf[0]
    for i in range(1, 16):
        degree = degree + gbuf[i]
    degree = jnp.broadcast_to(degree, (128, 40)).T[:, 0:1]
    o_ref[...] = total * scaled / degree

    for d in range(1, 4):
        a_out(d).wait_send()
    for i in range(3):
        pl.when(b_sends(i))(b_out(i).wait_send)
        d2_out(i).wait_send()
    for d in range(4):
        for e in range(1, 4):
            x_out(d, e).wait_send()
    for vv in range(4):

        @pl.when(vv != y)
        def _():
            for u2 in range(4):
                pl.when(tile_ok[u2])(r1_out(vv, u2).wait_send)

    for u2 in range(4):
        ok = jnp.logical_and(swap_ok[u2], jnp.logical_not(is_me(swap_to[u2])))
        pl.when(ok)(sw_out(u2).wait_send)
        for xx in range(4):
            ok = jnp.logical_and(own_ok[u2], jnp.logical_not(is_me(own_to[u2][xx])))
            pl.when(ok)(ow_out(u2, xx).wait_send)
    for i in range(15):
        d1_out(i).wait_send()
        g_out(i).wait_send()


def per_device(samples):
    rows, width = samples.shape
    total = 1.0 * rows * lax.axis_size("runs")
    scale = 4.0 * width * lax.axis_size("feat")
    dma = pltpu.SemaphoreType.DMA
    vm = pltpu.VMEM
    bf = jnp.bfloat16
    return pl.pallas_call(
        functools.partial(kernel, total, scale),
        out_shape=jax.ShapeDtypeStruct((rows, 4 * rows), F32),
        in_specs=[pl.BlockSpec(memory_space=pltpu.VMEM)],
        out_specs=pl.BlockSpec(memory_space=pltpu.VMEM),
        scratch_shapes=[
            vm((4, 4, rows, width), bf),
            vm((4, rows, width), bf),
            vm((4, 4 * rows, width), bf),
            vm((4 * rows, width), bf),
            vm((4, 4, rows, 4 * rows), F32),
            vm((4, 4, rows, 4 * rows), F32),
            vm((4, rows, 4 * rows), F32),
            vm((4, 4, rows, rows), F32),
            vm((2, rows, 4 * rows), F32),
            vm((2, 4, rows, rows), F32),
            vm((4, 4, 1, 4 * rows), F32),
            vm((4, 1, 4 * rows), F32),
            vm((16, 1, rows), F32),
            dma((4,)), dma((4,)),
            dma((4, 4)), dma((4, 4)),
            dma((3,)), dma((4,)),
            dma((4, 4)), dma((4, 4)),
            dma((4,)), dma((2,)),
            dma((4, 4)), dma((2, 4)),
            dma((15,)), dma((4, 4)),
            dma((3,)), dma((4,)),
            dma((15,)), dma((16,)),
        ],
        compiler_params=pltpu.CompilerParams(
            collective_id=0, has_side_effects=True, vmem_limit_bytes=48 << 20
        ),
        name="markov",
    )(samples)


def solution(mesh):
    placed = P("runs", "feat")
    return jax.shard_map(per_device, mesh=mesh, in_specs=(placed,), out_specs=placed, check_vma=False)
```

```python
import functools

import jax
import jax.numpy as jnp
from jax import lax
from jax.experimental import pallas as pl
from jax.experimental.pallas import tpu as pltpu
from jax.sharding import PartitionSpec as P

MESH = pl.DeviceIdType.MESH
F32 = jnp.float32
NT = (((1,), (1,)), ((), ()))


def device(x, z, y, h, c):
    return (z * 4 + x, (y * 2 + h) * 2 + c)


def kernel(
    total, scale, s_ref, o_ref, abuf, bbuf, acat, bcat, tbuf, r1buf, hsend, hbuf, swsend, owsend, swbuf, owbuf, d1buf, d2buf, gbuf,
    a_ss, a_rs, x_ss, x_rs, b_ss, b_rs, r1_ss, r1_rs, h_ss, h_rs, sw_ss, sw_rs, ow_ss, ow_rs, d1_ss, d1_rs, d2_ss, d2_rs, g_ss, g_rs,
):
    run, feat = lax.axis_index("runs"), lax.axis_index("feat")
    x, z = run % 4, run // 4
    u, v = z // 4, z % 4
    y, h, c = feat // 4, (feat // 2) % 2, feat % 2

    def copy(src, dst, ss, rs, to):
        return pltpu.make_async_remote_copy(
            src_ref=src, dst_ref=dst, send_sem=ss, recv_sem=rs, device_id=to, device_id_type=MESH
        )

    def is_me(to):
        return jnp.logical_and(to[0] == run, to[1] == feat)

    here = (run, feat)
    def nearest(other):
        return jnp.where(jnp.abs(other - u) == 3, 1 - h, h)

    swap_c = jnp.where(u <= y, 0, 1)
    own_c = jnp.where(y < u, 0, 1)
    swap_from = [device(x, y * 4 + v, 2 * b + c, nearest(y), swap_c) for b in range(2)]
    own_from = [[device(xx, u * 4 + 2 * b + c, v, h, own_c) for xx in range(4)] for b in range(2)]
    swap_ok = [jnp.where(c == 0, u2 <= u, u2 > u) for u2 in range(4)]
    own_ok = [jnp.where(c == 0, u2 < u, u2 >= u) for u2 in range(4)]
    tile_ok = [jnp.where(c == 0, u2 <= u, u2 >= u) for u2 in range(4)]
    swap_to = [device(x, u2 * 4 + v, u, nearest(u2), y % 2) for u2 in range(4)]
    own_to = [[device(xx, u * 4 + y, u2, h, v % 2) for xx in range(4)] for u2 in range(4)]

    near = [((x + dx) % 4, (v + dv) % 4) for dv in range(4) for dx in range(4) if (dx, dv) != (0, 0)]
    near_dev = [device(xx, u * 4 + vv, y, h, c) for xx, vv in near]
    us = [(u + d) % 4 for d in range(1, 4)]
    u_dev = [device(x, uu * 4 + v, y, h, c) for uu in us]
    other = device(x, z, y, 1 - h, c)
    plane = [((y + d // 2) % 4, (c + d) % 2) for d in range(1, 8)]
    plane_dev = [device(x, z, yy, h, cc) for yy, cc in plane]
    w = 4 * h + u
    ring_to = [(w + d) % 8 for d in (1, 7, 2)]
    ring_from = [(w + d) % 8 for d in (7, 1, 6)]
    ring_to_dev = [device(x, ww % 4 * 4 + v, y, ww // 4, c) for ww in ring_to]
    ring_from_dev = [device(x, ww % 4 * 4 + v, y, ww // 4, c) for ww in ring_from]

    barrier = pltpu.get_barrier_semaphore()
    for to in near_dev + u_dev + [other] + plane_dev + ring_from_dev:
        pl.semaphore_signal(barrier, inc=1, device_id=to, device_id_type=MESH)
    mine = 0
    for to in swap_from + own_from[0] + own_from[1]:
        same = is_me(to)
        mine = mine + jnp.where(same, 1, 0)

        @pl.when(jnp.logical_not(same))
        def _():
            pl.semaphore_signal(barrier, inc=1, device_id=to, device_id_type=MESH)

    pl.semaphore_wait(barrier, 29 + jnp.where(c == 0, 5 * u + 1, 19 - 5 * u) - mine)

    def b_out(i):
        return copy(s_ref, bbuf.at[u], b_ss.at[i], b_rs.at[u], u_dev[i])

    def b_sends(i):
        return jnp.where(c == 0, us[i] > u, us[i] < u)

    def a_out(d):
        return copy(s_ref, abuf.at[v, x], a_ss.at[d], a_rs.at[v], device(x, u * 4 + (v + d) % 4, y, h, c))

    def x_out(d, e):
        vv = (v + d) % 4
        src = s_ref if d == 0 else abuf.at[vv, x]
        return copy(src, abuf.at[vv, x], x_ss.at[d, e], x_rs.at[vv, x], device((x + e) % 4, z, y, h, c))

    for d in (1, 3, 2):
        a_out(d).start()
    for i in range(3):
        pl.when(b_sends(i))(b_out(i).start)
    for e in (1, 3, 2):
        x_out(0, e).start()
    abuf[v, x] = s_ref[...]
    bbuf[u] = s_ref[...]
    for d in (1, 3, 2):
        vv = (v + d) % 4
        copy(s_ref, abuf.at[vv, x], a_ss.at[d], a_rs.at[vv], here).wait_recv()
        for e in (1, 3, 2):
            x_out(d, e).start()
    for d in (0, 1, 3, 2):
        vv = (v + d) % 4
        for e in range(1, 4):
            xx = (x + e) % 4
            copy(s_ref, abuf.at[vv, xx], x_ss.at[d, e], x_rs.at[vv, xx], here).wait_recv()

    ones = jnp.ones((8, s_ref.shape[1]), jnp.bfloat16)
    norms = []
    for vv in range(4):
        wide = jnp.concatenate([abuf[vv, xx].astype(F32) for xx in range(4)], axis=0)
        acat[vv] = wide.astype(jnp.bfloat16)
        square = wide * wide
        high = square.astype(jnp.bfloat16)
        low = (square - high.astype(F32)).astype(jnp.bfloat16)
        norm = lax.dot_general(ones, high, NT, preferred_element_type=F32)
        norm = norm + lax.dot_general(ones, low, NT, preferred_element_type=F32)
        norms.append(norm[0:1])

    for i in range(3):
        uu = us[i]

        @pl.when(jnp.where(c == 0, uu < u, uu > u))
        def _():
            copy(s_ref, bbuf.at[uu], b_ss.at[i], b_rs.at[uu], here).wait_recv()

        @pl.when(jnp.where(c == 0, uu > u, uu < u))
        def _():
            bbuf[uu] = s_ref[...]

    wide = jnp.concatenate([bbuf[uu].astype(F32) for uu in range(4)], axis=0)
    bcat[...] = wide.astype(jnp.bfloat16)
    rownorm = jnp.sum(wide * wide, axis=1, keepdims=True)

    def r1_out(vv, k):
        return copy(tbuf.at[vv, k], r1buf.at[y, k], r1_ss.at[vv, k], r1_rs.at[y, k], device(x, z, vv, h, c))

    slot_ok = tile_ok + [u >= 0]
    for vv in range(4):
        gram = lax.dot_general(bcat[...], acat[vv], NT, preferred_element_type=F32)
        part = rownorm + norms[vv] - 2.0 * gram
        for u2 in range(4):
            tbuf[vv, u2] = part[u2 * 40 : u2 * 40 + 40, :128]
        tbuf[vv, 4] = jnp.concatenate([part[u2 * 40 : u2 * 40 + 40, 128:] for u2 in range(4)], axis=1)

        @pl.when(vv != y)
        def _():
            for k in range(5):
                pl.when(slot_ok[k])(r1_out(vv, k).start)

    def h_out(k):
        return copy(hsend.at[k], hbuf.at[k], h_ss.at[k], h_rs.at[k], other)

    for k in range(5):

        @pl.when(slot_ok[k])
        def _():
            for d in range(1, 4):
                yy = (y + d) % 4
                copy(tbuf.at[0, k], r1buf.at[yy, k], r1_ss.at[0, k], r1_rs.at[yy, k], here).wait_recv()
            tile = tbuf[y, k]
            for d in range(1, 4):
                tile = tile + r1buf[(y + d) % 4, k]
            hsend[k] = tile
            h_out(k).start()

    def sw_out(u2):
        return copy(swsend.at[u2], swbuf.at[y // 2], sw_ss.at[u2], sw_rs.at[y // 2], swap_to[u2])

    def ow_out(u2, xx):
        return copy(owsend.at[u2, xx], owbuf.at[v // 2, x], ow_ss.at[u2, xx], ow_rs.at[v // 2, x], own_to[u2][xx])

    copy(hsend.at[4], hbuf.at[4], h_ss.at[4], h_rs.at[4], other).wait_recv()
    rest = hsend[4] + hbuf[4]
    for u2 in range(4):

        @pl.when(tile_ok[u2])
        def _():
            copy(hsend.at[u2], hbuf.at[u2], h_ss.at[u2], h_rs.at[u2], other).wait_recv()
            tile = jnp.concatenate([hsend[u2] + hbuf[u2], rest[:, u2 * 32 : u2 * 32 + 32]], axis=1)
            swsend[u2] = tile
            turned = tile.T
            for xx in range(4):
                owsend[u2, xx] = turned[xx * 40 : xx * 40 + 40]

        same = is_me(swap_to[u2])

        @pl.when(jnp.logical_and(swap_ok[u2], same))
        def _():
            swbuf[y // 2] = swsend[u2]

        pl.when(jnp.logical_and(swap_ok[u2], jnp.logical_not(same)))(sw_out(u2).start)
        for xx in range(4):
            same = is_me(own_to[u2][xx])

            @pl.when(jnp.logical_and(own_ok[u2], same))
            def _():
                owbuf[v // 2, x] = owsend[u2, xx]

            pl.when(jnp.logical_and(own_ok[u2], jnp.logical_not(same)))(ow_out(u2, xx).start)

    for b in range(2):

        @pl.when(jnp.logical_not(is_me(swap_from[b])))
        def _():
            copy(swsend.at[0], swbuf.at[b], sw_ss.at[0], sw_rs.at[b], here).wait_recv()

        for xx in range(4):

            @pl.when(jnp.logical_not(is_me(own_from[b][xx])))
            def _():
                copy(owsend.at[0, 0], owbuf.at[b, xx], ow_ss.at[0, 0], ow_rs.at[b, xx], here).wait_recv()

    values = []
    for b in range(2):
        own = jnp.concatenate([owbuf[b, xx] for xx in range(4)], axis=1)
        values.append(jnp.exp(-(swbuf[b] + own) / scale))

    def d1_out(i):
        return copy(d1buf.at[v, x], d1buf.at[v, x], d1_ss.at[i], d1_rs.at[v, x], near_dev[i])

    for b in range(2):
        d1buf[v, x, b] = jnp.sum(values[b], axis=0, keepdims=True)
    for i in range(15):
        d1_out(i).start()
    for xx, vv in near:
        copy(d1buf.at[v, x], d1buf.at[vv, xx], d1_ss.at[0], d1_rs.at[vv, xx], here).wait_recv()
    density = d1buf[0, 0]
    for i in range(1, 16):
        density = density + d1buf[i // 4, i % 4]

    def d2_out(i):
        return copy(d2buf.at[u], d2buf.at[u], d2_ss.at[i], d2_rs.at[u], ring_to_dev[i])

    d2buf[u] = density
    for i in range(3):
        d2_out(i).start()
    for uu in us:
        copy(d2buf.at[u], d2buf.at[uu], d2_ss.at[0], d2_rs.at[uu], here).wait_recv()
    density = d2buf[0] + d2buf[1] + d2buf[2] + d2buf[3]

    scaled = [values[b] / density[b] for b in range(2)]
    degree = jnp.sum(scaled[0], axis=1, keepdims=True) + jnp.sum(scaled[1], axis=1, keepdims=True)
    place = 2 * y + c

    def g_out(i):
        return copy(gbuf.at[place], gbuf.at[place], g_ss.at[i], g_rs.at[place], plane_dev[i])

    gbuf[place] = jnp.broadcast_to(degree, (40, 128)).T[0:1]
    for i in range(7):
        g_out(i).start()
    for yy, cc in plane:
        copy(gbuf.at[place], gbuf.at[2 * yy + cc], g_ss.at[0], g_rs.at[2 * yy + cc], here).wait_recv()
    degree = gbuf[0]
    for i in range(1, 8):
        degree = degree + gbuf[i]
    degree = jnp.broadcast_to(degree, (128, 40)).T[:, 0:1]
    o_ref[...] = total * jnp.where(h == 0, scaled[0], scaled[1]) / degree

    for d in range(1, 4):
        a_out(d).wait_send()
    for i in range(3):
        pl.when(b_sends(i))(b_out(i).wait_send)
        d2_out(i).wait_send()
    for d in range(4):
        for e in range(1, 4):
            x_out(d, e).wait_send()
    for vv in range(4):

        @pl.when(vv != y)
        def _():
            for k in range(5):
                pl.when(slot_ok[k])(r1_out(vv, k).wait_send)

    for u2 in range(4):
        ok = jnp.logical_and(swap_ok[u2], jnp.logical_not(is_me(swap_to[u2])))
        pl.when(ok)(sw_out(u2).wait_send)
        for xx in range(4):
            ok = jnp.logical_and(own_ok[u2], jnp.logical_not(is_me(own_to[u2][xx])))
            pl.when(ok)(ow_out(u2, xx).wait_send)
    for k in range(5):
        pl.when(slot_ok[k])(h_out(k).wait_send)
    for i in range(15):
        d1_out(i).wait_send()
    for i in range(7):
        g_out(i).wait_send()


def per_device(samples):
    rows, width = samples.shape
    total = 1.0 * rows * lax.axis_size("runs")
    scale = 4.0 * width * lax.axis_size("feat")
    dma = pltpu.SemaphoreType.DMA
    vm = pltpu.VMEM
    bf = jnp.bfloat16
    return pl.pallas_call(
        functools.partial(kernel, total, scale),
        out_shape=jax.ShapeDtypeStruct((rows, 4 * rows), F32),
        in_specs=[pl.BlockSpec(memory_space=pltpu.VMEM)],
        out_specs=pl.BlockSpec(memory_space=pltpu.VMEM),
        scratch_shapes=[
            vm((4, 4, rows, width), bf),
            vm((4, rows, width), bf),
            vm((4, 4 * rows, width), bf),
            vm((4 * rows, width), bf),
            vm((4, 5, rows, 128), F32),
            vm((4, 5, rows, 128), F32),
            vm((5, rows, 128), F32),
            vm((5, rows, 128), F32),
            vm((4, rows, 4 * rows), F32),
            vm((4, 4, rows, rows), F32),
            vm((2, rows, 4 * rows), F32),
            vm((2, 4, rows, rows), F32),
            vm((4, 4, 2, 1, 4 * rows), F32),
            vm((4, 2, 1, 4 * rows), F32),
            vm((8, 1, rows), F32),
            dma((4,)), dma((4,)),
            dma((4, 4)), dma((4, 4)),
            dma((3,)), dma((4,)),
            dma((4, 5)), dma((4, 5)),
            dma((5,)), dma((5,)),
            dma((4,)), dma((2,)),
            dma((4, 4)), dma((2, 4)),
            dma((15,)), dma((4, 4)),
            dma((3,)), dma((4,)),
            dma((7,)), dma((8,)),
        ],
        compiler_params=pltpu.CompilerParams(
            collective_id=0, has_side_effects=True, vmem_limit_bytes=48 << 20
        ),
        name="markov",
    )(samples)


def solution(mesh):
    placed = P("runs", "feat")
    return jax.shard_map(per_device, mesh=mesh, in_specs=(placed,), out_specs=placed, check_vma=False)
```

```python
import functools

import jax
import jax.numpy as jnp
from jax import lax
from jax.experimental import pallas as pl
from jax.experimental.pallas import tpu as pltpu
from jax.sharding import PartitionSpec as P

MESH = pl.DeviceIdType.MESH
F32 = jnp.float32
BF16 = jnp.bfloat16
NT = (((1,), (1,)), ((), ()))


def device(x, z, y, h, c):
    return (z * 4 + x, (y * 2 + h) * 2 + c)


def pack(tile):
    rest = tile[:, 128:]
    first = jnp.concatenate([rest[i * 8 : i * 8 + 8] for i in range(4)], axis=1)
    second = jnp.concatenate([rest[32:40], jnp.zeros((8, 96), F32)], axis=1)
    return jnp.concatenate([tile[:, :128], first, second], axis=0)


def unpack(packed):
    rest = [packed[40:48, i * 32 : i * 32 + 32] for i in range(4)] + [packed[48:56, :32]]
    return jnp.concatenate([packed[:40], jnp.concatenate(rest, axis=0)], axis=1)


def kernel(
    total, scale, s_ref, o_ref, abuf, bbuf, acat, anorm, tbuf, r1buf, hsend, hbuf, swsend, owsend, swbuf, owbuf,
    d1buf, d2buf, gbuf, a_ss, a_rs, x_ss, x_rs, b_ss, b_rs, r1_ss, r1_rs, h_ss, h_rs, sw_ss, sw_rs, ow_ss, ow_rs,
    d1_ss, d1_rs, d2_ss, d2_rs, g_ss, g_rs, up_sem, down_sem, plane_sem,
):
    run, feat = lax.axis_index("runs"), lax.axis_index("feat")
    x, z = run % 4, run // 4
    u, v = z // 4, z % 4
    y, h, c = feat // 4, (feat // 2) % 2, feat % 2
    here = (run, feat)

    def copy(src, dst, ss, rs, to):
        return pltpu.make_async_remote_copy(
            src_ref=src, dst_ref=dst, send_sem=ss, recv_sem=rs, device_id=to, device_id_type=MESH
        )

    def signal(sem, to):
        pl.semaphore_signal(sem, inc=1, device_id=to, device_id_type=MESH)

    def is_me(to):
        return jnp.logical_and(to[0] == run, to[1] == feat)

    both = jnp.logical_and
    no = jnp.logical_not

    steps = jnp.where(c == 0, u + 1, 4 - u)
    way = jnp.where(c == 0, 1, -1)
    passes = jnp.where(c == 0, u < 3, u > 0)

    def u2(k):
        return u - way * k

    def nearest(other):
        return jnp.where(jnp.abs(other - u) == 3, 1 - h, h)

    swap_c = jnp.where(u <= y, 0, 1)
    own_c = jnp.where(y < u, 0, 1)
    swap_from = [device(x, y * 4 + v, 2 * b + c, nearest(y), swap_c) for b in range(2)]
    own_from = [[device(xx, u * 4 + 2 * b + c, v, h, own_c) for xx in range(4)] for b in range(2)]

    def swap_to(k):
        return device(x, u2(k) * 4 + v, u, nearest(u2(k)), y % 2)

    def own_to(k, xx):
        return device(xx, u * 4 + y, u2(k), h, v % 2)

    near = [((x + dx) % 4, (v + dv) % 4) for dv in range(4) for dx in range(4) if (dx, dv) != (0, 0)]
    near_dev = [device(xx, u * 4 + vv, y, h, c) for xx, vv in near]
    us = [(u + d) % 4 for d in range(1, 4)]
    other = device(x, z, y, 1 - h, c)
    plane = [((y + d // 2) % 4, (c + d) % 2) for d in range(1, 8)]
    plane_dev = [device(x, z, yy, h, cc) for yy, cc in plane]
    w = 4 * h + u
    ring = [(w + d) % 8 for d in (1, 7, 2)]
    above, below, above2 = [device(x, ww % 4 * 4 + v, y, ww // 4, c) for ww in ring]
    ring_to = [above, below, above2]

    barrier = pltpu.get_barrier_semaphore()
    for to in near_dev + [above, below] + plane_dev:
        signal(barrier, to)
    mine = 0
    for to in own_from[0] + own_from[1]:
        same = is_me(to)
        mine = mine + jnp.where(same, 1, 0)

        @pl.when(no(same))
        def _():
            signal(barrier, to)

    pl.semaphore_wait(barrier, 24 + 4 * jnp.where(c == 0, u, 4 - u) - mine)

    def b_out(k):
        src = s_ref if isinstance(k, int) and k == 0 else bbuf.at[u2(k)]
        to = device(x, (u + way) * 4 + v, y, h, c)
        return copy(src, bbuf.at[u2(k)], b_ss.at[k], b_rs.at[u2(k)], to)

    def b_in(k):
        return copy(s_ref, bbuf.at[u2(k)], b_ss.at[0], b_rs.at[u2(k)], here)

    def a_out(d):
        return copy(s_ref, abuf.at[v, x], a_ss.at[d], a_rs.at[v], device(x, u * 4 + (v + d) % 4, y, h, c))

    def x_out(d, e):
        vv = (v + d) % 4
        src = s_ref if d == 0 else abuf.at[vv, x]
        return copy(src, abuf.at[vv, x], x_ss.at[d, e], x_rs.at[vv, x], device((x + e) % 4, z, y, h, c))

    def relay_b(k):
        @pl.when(k < steps)
        def _():
            b_in(k).wait_recv()
            pl.when(passes)(b_out(k).start)

    def relay_a(d):
        vv = (v + d) % 4
        copy(s_ref, abuf.at[vv, x], a_ss.at[d], a_rs.at[vv], here).wait_recv()
        for e in (1, 3, 2):
            x_out(d, e).start()

    def take_a(d):
        vv = (v + d) % 4
        for e in range(1, 4):
            xx = (x + e) % 4
            copy(s_ref, abuf.at[vv, xx], x_ss.at[d, e], x_rs.at[vv, xx], here).wait_recv()
        wide = jnp.concatenate([abuf[vv, xx].astype(F32) for xx in range(4)], axis=0)
        acat[vv] = wide.astype(BF16)
        norm = jnp.sum(wide * wide, axis=1, keepdims=True)
        anorm[vv] = jnp.broadcast_to(norm, (norm.shape[0], 128)).T[0:1]

    pl.when(passes)(b_out(0).start)
    for d in (1, 3, 2):
        a_out(d).start()
    for e in (1, 3, 2):
        x_out(0, e).start()
    signal(up_sem, above)
    signal(down_sem.at[0], below)
    abuf[v, x] = s_ref[...]
    bbuf[u] = s_ref[...]
    relay_a(1)
    relay_a(3)
    pl.semaphore_wait(up_sem, 1)
    pl.semaphore_wait(down_sem.at[0], 1)
    signal(down_sem.at[1], below)
    for to in plane_dev:
        signal(plane_sem, to)
    relay_b(1)
    relay_a(2)
    take_a(0)
    pl.semaphore_wait(down_sem.at[1], 1)
    signal(down_sem.at[2], below)
    relay_b(2)
    take_a(1)
    take_a(3)
    take_a(2)

    pl.semaphore_wait(down_sem.at[2], 1)
    pl.semaphore_wait(plane_sem, 7)

    def r1_out(vv, k):
        return copy(tbuf.at[vv, k], r1buf.at[y, k], r1_ss.at[vv, k], r1_rs.at[y, k], device(x, z, vv, h, c))

    def h_out(k):
        return copy(hsend.at[k], hbuf.at[k], h_ss.at[k], h_rs.at[k], other)

    def reduce_y(k):
        for d in range(1, 4):
            yy = (y + d) % 4
            copy(tbuf.at[0, k], r1buf.at[yy, k], r1_ss.at[0, k], r1_rs.at[yy, k], here).wait_recv()
        tile = tbuf[y, k]
        for d in range(1, 4):
            tile = tile + r1buf[(y + d) % 4, k]
        hsend[k] = tile
        h_out(k).start()

    def tiles(k, carry):
        pl.when(k == 3)(lambda: b_in(k).wait_recv())
        block = bbuf[u2(k)]
        wide = block.astype(F32)
        norm = jnp.sum(wide * wide, axis=1, keepdims=True)
        for vv in range(4):
            gram = lax.dot_general(block, acat[vv], NT, preferred_element_type=F32)
            tbuf[vv, k] = pack(norm + anorm[vv] - 2.0 * gram)
            pl.when(vv != y)(r1_out(vv, k).start)
        pl.when(k > 0)(lambda: reduce_y(k - 1))
        return carry

    lax.fori_loop(0, steps, tiles, 0)
    reduce_y(steps - 1)

    def sw_out(k):
        return copy(swsend.at[k], swbuf.at[y // 2], sw_ss.at[k], sw_rs.at[y // 2], swap_to(k))

    def ow_out(k, xx):
        return copy(owsend.at[k, xx], owbuf.at[v // 2, x], ow_ss.at[k, xx], ow_rs.at[v // 2, x], own_to(k, xx))

    def swaps(k):
        return jnp.logical_or(c == 0, k > 0)

    def owns(k):
        return jnp.logical_or(c == 1, k > 0)

    def place(k, carry):
        copy(hsend.at[k], hbuf.at[k], h_ss.at[k], h_rs.at[k], other).wait_recv()
        packed = hsend[k] + hbuf[k]
        swsend[k] = packed
        same = is_me(swap_to(k))

        @pl.when(both(swaps(k), same))
        def _():
            swbuf[y // 2] = swsend[k]

        pl.when(both(swaps(k), no(same)))(sw_out(k).start)

        @pl.when(owns(k))
        def _():
            turned = unpack(packed).T
            for xx in range(4):
                owsend[k, xx] = turned[xx * 40 : xx * 40 + 40]
                same = is_me(own_to(k, xx))

                @pl.when(same)
                def _():
                    owbuf[v // 2, x] = owsend[k, xx]

                pl.when(no(same))(ow_out(k, xx).start)

        return carry

    lax.fori_loop(0, steps, place, 0)

    for b in range(2):

        @pl.when(no(is_me(swap_from[b])))
        def _():
            copy(swsend.at[0], swbuf.at[b], sw_ss.at[0], sw_rs.at[b], here).wait_recv()

        for xx in range(4):

            @pl.when(no(is_me(own_from[b][xx])))
            def _():
                copy(owsend.at[0, 0], owbuf.at[b, xx], ow_ss.at[0, 0], ow_rs.at[b, xx], here).wait_recv()

    values = []
    for b in range(2):
        own = jnp.concatenate([owbuf[b, xx] for xx in range(4)], axis=1)
        values.append(jnp.exp(-(unpack(swbuf[b]) + own) / scale))

    def d1_out(i):
        return copy(d1buf.at[v, x], d1buf.at[v, x], d1_ss.at[i], d1_rs.at[v, x], near_dev[i])

    for b in range(2):
        d1buf[v, x, b] = jnp.sum(values[b], axis=0, keepdims=True)
    for i in range(15):
        d1_out(i).start()
    for xx, vv in near:
        copy(d1buf.at[v, x], d1buf.at[vv, xx], d1_ss.at[0], d1_rs.at[vv, xx], here).wait_recv()
    density = d1buf[0, 0]
    for i in range(1, 16):
        density = density + d1buf[i // 4, i % 4]

    def d2_out(i):
        return copy(d2buf.at[u], d2buf.at[u], d2_ss.at[i], d2_rs.at[u], ring_to[i])

    d2buf[u] = density
    for i in range(3):
        d2_out(i).start()
    for uu in us:
        copy(d2buf.at[u], d2buf.at[uu], d2_ss.at[0], d2_rs.at[uu], here).wait_recv()
    density = d2buf[0] + d2buf[1] + d2buf[2] + d2buf[3]

    scaled = [values[b] / density[b] for b in range(2)]
    degree = jnp.sum(scaled[0], axis=1, keepdims=True) + jnp.sum(scaled[1], axis=1, keepdims=True)
    place = 2 * y + c

    def g_out(i):
        return copy(gbuf.at[place], gbuf.at[place], g_ss.at[i], g_rs.at[place], plane_dev[i])

    gbuf[place] = jnp.broadcast_to(degree, (40, 128)).T[0:1]
    for i in range(7):
        g_out(i).start()
    for yy, cc in plane:
        copy(gbuf.at[place], gbuf.at[2 * yy + cc], g_ss.at[0], g_rs.at[2 * yy + cc], here).wait_recv()
    degree = gbuf[0]
    for i in range(1, 8):
        degree = degree + gbuf[i]
    degree = jnp.broadcast_to(degree, (128, 40)).T[:, 0:1]
    o_ref[...] = total * jnp.where(h == 0, scaled[0], scaled[1]) / degree

    for d in range(1, 4):
        a_out(d).wait_send()
    for d in range(4):
        for e in range(1, 4):
            x_out(d, e).wait_send()
    for k in range(3):
        pl.when(both(passes, k < steps))(b_out(k).wait_send)

    def sent_tiles(k, carry):
        for vv in range(4):
            pl.when(vv != y)(r1_out(vv, k).wait_send)
        h_out(k).wait_send()
        return carry

    lax.fori_loop(0, steps, sent_tiles, 0)

    def sent_places(k, carry):
        pl.when(both(swaps(k), no(is_me(swap_to(k)))))(sw_out(k).wait_send)
        for xx in range(4):
            pl.when(both(owns(k), no(is_me(own_to(k, xx)))))(ow_out(k, xx).wait_send)
        return carry

    lax.fori_loop(0, steps, sent_places, 0)

    for i in range(15):
        d1_out(i).wait_send()
    for i in range(3):
        d2_out(i).wait_send()

    for i in range(7):
        g_out(i).wait_send()


def per_device(samples):
    rows, width = samples.shape
    total = 1.0 * rows * lax.axis_size("runs")
    scale = 4.0 * width * lax.axis_size("feat")
    dma = pltpu.SemaphoreType.DMA
    regular = pltpu.SemaphoreType.REGULAR
    vm = pltpu.VMEM
    return pl.pallas_call(
        functools.partial(kernel, total, scale),
        out_shape=jax.ShapeDtypeStruct((rows, 4 * rows), F32),
        in_specs=[pl.BlockSpec(memory_space=pltpu.VMEM)],
        out_specs=pl.BlockSpec(memory_space=pltpu.VMEM),
        scratch_shapes=[
            vm((4, 4, rows, width), BF16),
            vm((4, rows, width), BF16),
            vm((4, 4 * rows, width), BF16),
            vm((4, 1, 4 * rows), F32),
            vm((4, 4, 56, 128), F32),
            vm((4, 4, 56, 128), F32),
            vm((4, 56, 128), F32),
            vm((4, 56, 128), F32),
            vm((4, 56, 128), F32),
            vm((4, 4, rows, rows), F32),
            vm((2, 56, 128), F32),
            vm((2, 4, rows, rows), F32),
            vm((4, 4, 2, 1, 4 * rows), F32),
            vm((4, 2, 1, 4 * rows), F32),
            vm((8, 1, rows), F32),
            dma((4,)), dma((4,)),
            dma((4, 4)), dma((4, 4)),
            dma((3,)), dma((4,)),
            dma((4, 4)), dma((4, 4)),
            dma((4,)), dma((4,)),
            dma((4,)), dma((2,)),
            dma((4, 4)), dma((2, 4)),
            dma((15,)), dma((4, 4)),
            dma((3,)), dma((4,)),
            dma((7,)), dma((8,)),
            regular, regular((3,)), regular,
        ],
        compiler_params=pltpu.CompilerParams(
            collective_id=0, has_side_effects=True, vmem_limit_bytes=48 << 20
        ),
        name="markov",
    )(samples)


def solution(mesh):
    placed = P("runs", "feat")
    return jax.shard_map(per_device, mesh=mesh, in_specs=(placed,), out_specs=placed, check_vma=False)
```

```python
import functools

import jax
import jax.numpy as jnp
from jax import lax
from jax.experimental import pallas as pl
from jax.experimental.pallas import tpu as pltpu
from jax.sharding import PartitionSpec as P

MESH = pl.DeviceIdType.MESH
F32 = jnp.float32
BF16 = jnp.bfloat16
NT = (((1,), (1,)), ((), ()))


def device(x, z, y, h, c):
    return (z * 4 + x, (y * 2 + h) * 2 + c)


def pack(tile):
    last = jnp.concatenate([tile[112:], jnp.zeros((8, 40), F32)], axis=0)
    return jnp.concatenate([tile[:56], tile[56:112], last, jnp.zeros((56, 8), F32)], axis=1)


def unpack(packed):
    return jnp.concatenate([packed[:, :40], packed[:, 40:80], packed[:48, 80:120]], axis=0)


def pack_quarter(part):
    first = jnp.concatenate([part[:8], part[8:16], part[16:24], jnp.zeros((8, 8), F32)], axis=1)
    second = jnp.concatenate([part[24:32], part[32:], jnp.zeros((8, 48), F32)], axis=1)
    return jnp.concatenate([first, second], axis=0)


def unpack_quarter(packed):
    pieces = [packed[:8, i * 40 : i * 40 + 40] for i in range(3)] + [packed[8:, i * 40 : i * 40 + 40] for i in range(2)]
    return jnp.concatenate(pieces, axis=0)


def kernel(
    total, scale, s_ref, o_ref, abuf, bbuf, acat, anorm, bnorm, tbuf, r1buf, hsend, hbuf, swsend, owsend, swbuf, owbuf,
    d1buf, d2buf, gbuf, a_ss, a_rs, x_ss, x_rs, b_ss, b_rs, r1_ss, r1_rs, h_ss, h_rs, sw_ss, sw_rs, ow_ss, ow_rs,
    d1_ss, d1_rs, d2_ss, d2_rs, g_ss, g_rs, up_sem, down_sem, plane_sem, side_sem,
    near_sem, in_sem,
):
    run, feat = lax.axis_index("runs"), lax.axis_index("feat")
    x, z = run % 4, run // 4
    u, v = z // 4, z % 4
    y, h, c = feat // 4, (feat // 2) % 2, feat % 2
    here = (run, feat)

    def copy(src, dst, ss, rs, to):
        return pltpu.make_async_remote_copy(
            src_ref=src, dst_ref=dst, send_sem=ss, recv_sem=rs, device_id=to, device_id_type=MESH
        )

    def signal(sem, to):
        pl.semaphore_signal(sem, inc=1, device_id=to, device_id_type=MESH)

    def is_me(to):
        return jnp.logical_and(to[0] == run, to[1] == feat)

    both = jnp.logical_and
    no = jnp.logical_not

    steps = jnp.where(c == 0, u + 1, 4 - u)
    way = jnp.where(c == 0, 1, -1)
    passes = jnp.where(c == 0, u < 3, u > 0)

    def u2(k):
        return u - way * k

    def nearest(other):
        return jnp.where(jnp.abs(other - u) == 3, 1 - h, h)

    swap_c = jnp.where(u <= y, 0, 1)
    own_c = jnp.where(y < u, 0, 1)
    swap_from = [device(x, y * 4 + v, 2 * b + c, nearest(y), swap_c) for b in range(2)]
    own_from = [[device(xx, u * 4 + 2 * b + c, v, h, own_c) for xx in range(4)] for b in range(2)]

    def swap_to(k):
        return device(x, u2(k) * 4 + v, u, nearest(u2(k)), y % 2)

    def own_to(k, xx):
        return device(xx, u * 4 + y, u2(k), h, v % 2)

    near = [((x + dx) % 4, (v + dv) % 4) for dv in range(4) for dx in range(4) if (dx, dv) != (0, 0)]
    near_dev = [device(xx, u * 4 + vv, y, h, c) for xx, vv in near]
    other = device(x, z, y, 1 - h, c)
    plane = [((y + d // 2) % 4, (c + d) % 2) for d in range(1, 8)]
    plane_dev = [device(x, z, yy, h, cc) for yy, cc in plane]
    w = 4 * h + u
    ring = [(w + d) % 8 for d in (1, 7, 2)]
    above, below, above2 = [device(x, ww % 4 * 4 + v, y, ww // 4, c) for ww in ring]
    ring_to = [above, below, above2]

    load = pltpu.make_async_copy(s_ref, abuf.at[v, x], in_sem)
    load.start()
    side_dev = [device((x + d) % 4, z, y, h, c) for d in range(1, 4)]
    line_dev = [device(x, u * 4 + (v + d) % 4, y, h, c) for d in range(1, 4)]
    barrier = pltpu.get_barrier_semaphore()
    for to in [above, below] + line_dev + side_dev + plane_dev:
        signal(barrier, to)
    load.wait()
    pl.semaphore_wait(barrier, 15)

    mine = abuf.at[v, x]

    def b_out(k):
        src = mine if isinstance(k, int) and k == 0 else bbuf.at[u2(k)]
        to = device(x, (u + way) * 4 + v, y, h, c)
        return copy(src, bbuf.at[u2(k)], b_ss.at[k], b_rs.at[u2(k)], to)

    def b_in(k):
        return copy(mine, bbuf.at[u2(k)], b_ss.at[0], b_rs.at[u2(k)], here)

    def a_out(d):
        return copy(mine, abuf.at[v, x], a_ss.at[d], a_rs.at[v], device(x, u * 4 + (v + d) % 4, y, h, c))

    def x_out(d, e):
        vv = (v + d) % 4
        src = abuf.at[vv, x]
        return copy(src, abuf.at[vv, x], x_ss.at[d, e], x_rs.at[vv, x], device((x + e) % 4, z, y, h, c))

    def relay_b(k):
        @pl.when(k < steps)
        def _():
            b_in(k).wait_recv()
            pl.when(passes)(b_out(k).start)

    def relay_a(d):
        vv = (v + d) % 4
        copy(mine, abuf.at[vv, x], a_ss.at[d], a_rs.at[vv], here).wait_recv()
        for e in (1, 3, 2):
            x_out(d, e).start()

    def take_a(d):
        vv = (v + d) % 4
        for e in range(1, 4):
            xx = (x + e) % 4
            copy(mine, abuf.at[vv, xx], x_ss.at[d, e], x_rs.at[vv, xx], here).wait_recv()
        wide = jnp.concatenate([abuf[vv, xx].astype(F32) for xx in range(4)], axis=0)
        acat[vv] = wide.astype(BF16)
        norm = jnp.sum(wide * wide, axis=1, keepdims=True)
        anorm[vv] = jnp.broadcast_to(norm, (norm.shape[0], 128))

    pl.when(passes)(b_out(0).start)
    for d in (1, 3, 2):
        a_out(d).start()
    for e in (1, 3, 2):
        x_out(0, e).start()
    signal(up_sem, above)
    signal(down_sem.at[0], below)
    for to in side_dev:
        signal(side_sem, to)
    bbuf[u] = abuf[v, x]
    relay_a(1)
    relay_b(1)
    relay_a(3)
    relay_a(2)
    pl.semaphore_wait(side_sem, 3)
    for to in near_dev:
        signal(near_sem, to)
    pl.semaphore_wait(up_sem, 1)
    pl.semaphore_wait(down_sem.at[0], 1)
    signal(down_sem.at[1], below)
    for to in plane_dev:
        signal(plane_sem, to)
    def r1_out(vv, k):
        return copy(tbuf.at[vv, k], r1buf.at[y, k], r1_ss.at[vv, k], r1_rs.at[y, k], device(x, z, vv, h, c))

    def h_out(k):
        return copy(hsend.at[k], hbuf.at[k], h_ss.at[k], h_rs.at[k], other)

    def reduce_y(k):
        for d in range(1, 4):
            yy = (y + d) % 4
            copy(tbuf.at[0, k], r1buf.at[yy, k], r1_ss.at[0, k], r1_rs.at[yy, k], here).wait_recv()
        tile = tbuf[y, k]
        for d in range(1, 4):
            tile = tile + r1buf[(y + d) % 4, k]
        hsend[k] = tile
        h_out(k).start()

    def norm_of(k):
        wide = bbuf[u2(k)].astype(F32)
        norm = jnp.sum(wide * wide, axis=1, keepdims=True)
        bnorm[k] = jnp.broadcast_to(norm, (norm.shape[0], 128)).T[0:1]

    def tile(k, d):
        vv = (v + d) % 4
        gram = lax.dot_general(acat[vv], bbuf[u2(k)], NT, preferred_element_type=F32)
        tbuf[vv, k] = pack(bnorm[k] + anorm[vv, :, :40] - 2.0 * gram)
        pl.when(vv != y)(r1_out(vv, k).start)

    def tiles(first, last, ds):
        def one(k, carry):
            for d in ds:
                tile(k, d)
            return carry

        lax.fori_loop(first, last, one, 0)

    def reduce_all(first, last):
        def one(k, carry):
            reduce_y(k)
            return carry

        lax.fori_loop(first, last, one, 0)

    three_steps = jnp.minimum(steps, 3)

    def reduce_if(d):
        pl.when((v + d) % 4 == y)(lambda: reduce_all(0, three_steps))

    pl.semaphore_wait(down_sem.at[1], 1)
    signal(down_sem.at[2], below)
    relay_b(2)
    take_a(0)
    for k in range(3):
        pl.when(k < steps)(functools.partial(norm_of, k))
    tiles(0, three_steps, (0,))
    take_a(1)
    tiles(0, three_steps, (1,))
    pl.semaphore_wait(down_sem.at[2], 1)
    reduce_if(0)
    take_a(3)
    tiles(0, three_steps, (3,))
    reduce_if(1)
    take_a(2)
    tiles(0, three_steps, (2,))
    reduce_if(3)
    pl.semaphore_wait(plane_sem, 7)
    pl.semaphore_wait(near_sem, 15)

    @pl.when(steps == 4)
    def _():
        b_in(3).wait_recv()
        norm_of(3)
        tiles(3, 4, (0, 1, 3, 2))

    reduce_if(2)
    pl.when(steps == 4)(lambda: reduce_all(3, 4))

    def sw_out(k):
        return copy(swsend.at[k], swbuf.at[y // 2], sw_ss.at[k], sw_rs.at[y // 2], swap_to(k))

    def ow_out(k, xx):
        return copy(owsend.at[k, xx], owbuf.at[v // 2, x], ow_ss.at[k, xx], ow_rs.at[v // 2, x], own_to(k, xx))

    def swaps(k):
        return jnp.logical_or(c == 0, k > 0)

    def owns(k):
        return jnp.logical_or(c == 1, k > 0)

    def place(k, carry):
        copy(hsend.at[k], hbuf.at[k], h_ss.at[k], h_rs.at[k], other).wait_recv()
        packed = hsend[k] + hbuf[k]
        swsend[k] = packed
        same = is_me(swap_to(k))

        @pl.when(both(swaps(k), same))
        def _():
            swbuf[y // 2] = swsend[k]

        pl.when(both(swaps(k), no(same)))(sw_out(k).start)

        @pl.when(owns(k))
        def _():
            turned = unpack(packed)
            for xx in range(4):
                owsend[k, xx] = pack_quarter(turned[xx * 40 : xx * 40 + 40])
                same = is_me(own_to(k, xx))

                @pl.when(same)
                def _():
                    owbuf[v // 2, x] = owsend[k, xx]

                pl.when(no(same))(ow_out(k, xx).start)

        return carry

    lax.fori_loop(0, steps, place, 0)

    for b in range(2):

        @pl.when(no(is_me(swap_from[b])))
        def _():
            copy(swsend.at[0], swbuf.at[b], sw_ss.at[0], sw_rs.at[b], here).wait_recv()

        for xx in range(4):

            @pl.when(no(is_me(own_from[b][xx])))
            def _():
                copy(owsend.at[0, 0], owbuf.at[b, xx], ow_ss.at[0, 0], ow_rs.at[b, xx], here).wait_recv()

    values = []
    for b in range(2):
        own = jnp.concatenate([unpack_quarter(owbuf[b, xx]) for xx in range(4)], axis=1)
        values.append(jnp.exp(-(unpack(swbuf[b]).T + own) / scale))

    def d1_out(i):
        return copy(d1buf.at[4 * v + x], d1buf.at[4 * v + x], d1_ss, d1_rs, near_dev[i])

    for b in range(2):
        d1buf[4 * v + x, b] = jnp.sum(values[b], axis=0, keepdims=True)
    for i in range(15):
        d1_out(i).start()
    fifteen = d1buf.at[pl.ds(0, 15)]
    copy(fifteen, fifteen, d1_ss, d1_rs, here).wait_recv()
    density = d1buf[0]
    for i in range(1, 16):
        density = density + d1buf[i]

    def d2_out(i):
        return copy(d2buf.at[u], d2buf.at[u], d2_ss, d2_rs, ring_to[i])

    d2buf[u] = density
    for i in range(3):
        d2_out(i).start()
    three = d2buf.at[pl.ds(0, 3)]
    copy(three, three, d2_ss, d2_rs, here).wait_recv()
    density = d2buf[0] + d2buf[1] + d2buf[2] + d2buf[3]

    scaled = [values[b] / density[b] for b in range(2)]
    degree = jnp.sum(scaled[0], axis=1, keepdims=True) + jnp.sum(scaled[1], axis=1, keepdims=True)
    place = 2 * y + c

    def g_out(i):
        return copy(gbuf.at[place], gbuf.at[place], g_ss, g_rs, plane_dev[i])

    gbuf[place] = jnp.broadcast_to(degree, (40, 128)).T[0:1]
    for i in range(7):
        g_out(i).start()
    for d in range(1, 4):
        a_out(d).wait_send()
    for d in range(4):
        for e in range(1, 4):
            x_out(d, e).wait_send()
    for k in range(3):
        pl.when(both(passes, k < steps))(b_out(k).wait_send)

    def sent_tiles(k, carry):
        for vv in range(4):
            pl.when(vv != y)(r1_out(vv, k).wait_send)
        h_out(k).wait_send()
        return carry

    lax.fori_loop(0, steps, sent_tiles, 0)

    def sent_places(k, carry):
        pl.when(both(swaps(k), no(is_me(swap_to(k)))))(sw_out(k).wait_send)
        for xx in range(4):
            pl.when(both(owns(k), no(is_me(own_to(k, xx)))))(ow_out(k, xx).wait_send)
        return carry

    lax.fori_loop(0, steps, sent_places, 0)

    copy(fifteen, fifteen, d1_ss, d1_rs, here).wait_send()
    copy(three, three, d2_ss, d2_rs, here).wait_send()

    seven = gbuf.at[pl.ds(0, 7)]
    copy(seven, seven, g_ss, g_rs, here).wait_recv()
    degree = gbuf[0]
    for i in range(1, 8):
        degree = degree + gbuf[i]
    degree = jnp.broadcast_to(degree, (128, 40)).T[:, 0:1]
    o_ref[...] = total * jnp.where(h == 0, scaled[0], scaled[1]) / degree

    copy(seven, seven, g_ss, g_rs, here).wait_send()


def per_device(samples):
    rows, width = samples.shape
    total = 1.0 * rows * lax.axis_size("runs")
    scale = 4.0 * width * lax.axis_size("feat")
    dma = pltpu.SemaphoreType.DMA
    regular = pltpu.SemaphoreType.REGULAR
    vm = pltpu.VMEM
    return pl.pallas_call(
        functools.partial(kernel, total, scale),
        out_shape=jax.ShapeDtypeStruct((rows, 4 * rows), F32),
        in_specs=[pl.BlockSpec(memory_space=pl.ANY)],
        out_specs=pl.BlockSpec(memory_space=pltpu.VMEM),
        scratch_shapes=[
            vm((4, 4, rows, width), BF16),
            vm((4, rows, width), BF16),
            vm((4, 4 * rows, width), BF16),
            vm((4, 4 * rows, 128), F32),
            vm((4, 1, rows), F32),
            vm((4, 4, 56, 128), F32),
            vm((4, 4, 56, 128), F32),
            vm((4, 56, 128), F32),
            vm((4, 56, 128), F32),
            vm((4, 56, 128), F32),
            vm((4, 4, 16, 128), F32),
            vm((2, 56, 128), F32),
            vm((2, 4, 16, 128), F32),
            vm((16, 2, 1, 4 * rows), F32),
            vm((4, 2, 1, 4 * rows), F32),
            vm((8, 1, rows), F32),
            dma((4,)), dma((4,)),
            dma((4, 4)), dma((4, 4)),
            dma((3,)), dma((4,)),
            dma((4, 4)), dma((4, 4)),
            dma((4,)), dma((4,)),
            dma((4,)), dma((2,)),
            dma((4, 4)), dma((2, 4)),
            dma, dma,
            dma, dma,
            dma, dma,
            regular, regular((3,)), regular, regular, regular, dma,
        ],
        compiler_params=pltpu.CompilerParams(
            collective_id=0, has_side_effects=True, vmem_limit_bytes=48 << 20
        ),
        name="markov",
    )(samples)


def solution(mesh):
    placed = P("runs", "feat")
    return jax.shard_map(per_device, mesh=mesh, in_specs=(placed,), out_specs=placed, check_vma=False)
```

```python
import functools

import jax
import jax.numpy as jnp
from jax import lax
from jax.experimental import pallas as pl
from jax.experimental.pallas import tpu as pltpu
from jax.sharding import PartitionSpec as P

MESH = pl.DeviceIdType.MESH
F32 = jnp.float32
BF16 = jnp.bfloat16
NT = (((1,), (1,)), ((), ()))


def device(x, z, y, h, c):
    return (z * 4 + x, (y * 2 + h) * 2 + c)


def pack(tile):
    last = jnp.concatenate([tile[112:], jnp.zeros((8, 40), F32)], axis=0)
    return jnp.concatenate([tile[:56], tile[56:112], last, jnp.zeros((56, 8), F32)], axis=1)


def unpack(packed):
    return jnp.concatenate([packed[:, :40], packed[:, 40:80], packed[:48, 80:120]], axis=0)


def pack_quarter(part):
    first = jnp.concatenate([part[:8], part[8:16], part[16:24], jnp.zeros((8, 8), F32)], axis=1)
    second = jnp.concatenate([part[24:32], part[32:], jnp.zeros((8, 48), F32)], axis=1)
    return jnp.concatenate([first, second], axis=0)


def unpack_quarter(packed):
    pieces = [packed[:8, i * 40 : i * 40 + 40] for i in range(3)] + [packed[8:, i * 40 : i * 40 + 40] for i in range(2)]
    return jnp.concatenate(pieces, axis=0)


def kernel(
    total, scale, s_ref, o_ref, abuf, bbuf, acat, anorm, bnorm, tbuf, r1buf, hsend, hbuf, swsend, owsend, swbuf, owbuf,
    d1buf, d2buf, gbuf, a_ss, a_rs, x_ss, x_rs, b_ss, b_rs, r1_ss, r1_rs, h_ss, h_rs, sw_ss, sw_rs, ow_ss, ow_rs,
    d1_ss, d1_rs, d2_ss, d2_rs, g_ss, g_rs, up_sem, down_sem, plane_sem, side_sem,
    near_sem, in_sem,
):
    run, feat = lax.axis_index("runs"), lax.axis_index("feat")
    x, z = run % 4, run // 4
    u, v = z // 4, z % 4
    y, h, c = feat // 4, (feat // 2) % 2, feat % 2
    here = (run, feat)

    def copy(src, dst, ss, rs, to):
        return pltpu.make_async_remote_copy(
            src_ref=src, dst_ref=dst, send_sem=ss, recv_sem=rs, device_id=to, device_id_type=MESH
        )

    def signal(sem, to):
        pl.semaphore_signal(sem, inc=1, device_id=to, device_id_type=MESH)

    def is_me(to):
        return jnp.logical_and(to[0] == run, to[1] == feat)

    both = jnp.logical_and
    no = jnp.logical_not

    steps = jnp.where(c == 0, u + 1, 4 - u)
    way = jnp.where(c == 0, 1, -1)
    passes = jnp.where(c == 0, u < 3, u > 0)

    def u2(k):
        return u - way * k

    def nearest(other):
        return jnp.where(jnp.abs(other - u) == 3, 1 - h, h)

    swap_c = jnp.where(u <= y, 0, 1)
    own_c = jnp.where(y < u, 0, 1)
    swap_from = [device(x, y * 4 + v, 2 * b + c, nearest(y), swap_c) for b in range(2)]
    own_from = [[device(xx, u * 4 + 2 * b + c, v, h, own_c) for xx in range(4)] for b in range(2)]

    def swap_to(k):
        return device(x, u2(k) * 4 + v, u, nearest(u2(k)), y % 2)

    def own_to(k, xx):
        return device(xx, u * 4 + y, u2(k), h, v % 2)

    near = [((x + dx) % 4, (v + dv) % 4) for dv in range(4) for dx in range(4) if (dx, dv) != (0, 0)]
    near_dev = [device(xx, u * 4 + vv, y, h, c) for xx, vv in near]
    other = device(x, z, y, 1 - h, c)
    plane = [((y + d // 2) % 4, (c + d) % 2) for d in range(1, 8)]
    plane_dev = [device(x, z, yy, h, cc) for yy, cc in plane]
    w = 4 * h + u
    ring = [(w + d) % 8 for d in (1, 7, 2)]
    above, below, above2 = [device(x, ww % 4 * 4 + v, y, ww // 4, c) for ww in ring]
    ring_to = [above, below, above2]

    load = pltpu.make_async_copy(s_ref, abuf.at[v, x], in_sem)
    load.start()
    side_dev = [device((x + d) % 4, z, y, h, c) for d in range(1, 4)]
    line_dev = [device(x, u * 4 + (v + d) % 4, y, h, c) for d in range(1, 4)]
    barrier = pltpu.get_barrier_semaphore()
    for to in [above, below] + line_dev + side_dev + plane_dev:
        signal(barrier, to)
    load.wait()
    pl.semaphore_wait(barrier, 15)

    mine = abuf.at[v, x]

    def b_out(k):
        src = mine if isinstance(k, int) and k == 0 else bbuf.at[u2(k)]
        to = device(x, (u + way) * 4 + v, y, h, c)
        return copy(src, bbuf.at[u2(k)], b_ss.at[k], b_rs.at[u2(k)], to)

    def b_in(k):
        return copy(mine, bbuf.at[u2(k)], b_ss.at[0], b_rs.at[u2(k)], here)

    def a_out(d):
        return copy(mine, abuf.at[v, x], a_ss.at[d], a_rs.at[v], device(x, u * 4 + (v + d) % 4, y, h, c))

    def x_out(d, e):
        vv = (v + d) % 4
        src = abuf.at[vv, x]
        return copy(src, abuf.at[vv, x], x_ss.at[d, e], x_rs.at[vv, x], device((x + e) % 4, z, y, h, c))

    def relay_b(k):
        @pl.when(k < steps)
        def _():
            b_in(k).wait_recv()
            pl.when(passes)(b_out(k).start)

    def relay_a(d):
        vv = (v + d) % 4
        copy(mine, abuf.at[vv, x], a_ss.at[d], a_rs.at[vv], here).wait_recv()
        for e in (1, 3, 2):
            x_out(d, e).start()

    def take_a(d):
        vv = (v + d) % 4
        for e in range(1, 4):
            xx = (x + e) % 4
            copy(mine, abuf.at[vv, xx], x_ss.at[d, e], x_rs.at[vv, xx], here).wait_recv()
        wide = jnp.concatenate([abuf[vv, xx].astype(F32) for xx in range(4)], axis=0)
        acat[vv] = wide.astype(BF16)
        norm = jnp.sum(wide * wide, axis=1, keepdims=True)
        anorm[vv] = jnp.broadcast_to(norm, (norm.shape[0], 128))

    pl.when(passes)(b_out(0).start)
    for d in (1, 3, 2):
        a_out(d).start()
    for e in (1, 3, 2):
        x_out(0, e).start()
    signal(up_sem, above)
    signal(down_sem.at[0], below)
    for to in side_dev:
        signal(side_sem, to)
    bbuf[u] = abuf[v, x]
    relay_a(1)
    relay_b(1)
    relay_a(3)
    relay_a(2)
    pl.semaphore_wait(side_sem, 3)
    for to in near_dev:
        signal(near_sem, to)
    pl.semaphore_wait(up_sem, 1)
    pl.semaphore_wait(down_sem.at[0], 1)
    signal(down_sem.at[1], below)
    for to in plane_dev:
        signal(plane_sem, to)
    def r1_out(vv, k):
        return copy(tbuf.at[vv, k], r1buf.at[y, k], r1_ss.at[vv, k], r1_rs.at[y, k], device(x, z, vv, h, c))

    def h_out(k):
        return copy(hsend.at[k], hbuf.at[k], h_ss.at[k], h_rs.at[k], other)

    def reduce_y(k):
        for d in range(1, 4):
            yy = (y + d) % 4
            copy(tbuf.at[0, k], r1buf.at[yy, k], r1_ss.at[0, k], r1_rs.at[yy, k], here).wait_recv()
        tile = tbuf[y, k]
        for d in range(1, 4):
            tile = tile + r1buf[(y + d) % 4, k]
        hsend[k] = tile
        h_out(k).start()

    def norm_of(k):
        wide = bbuf[u2(k)].astype(F32)
        norm = jnp.sum(wide * wide, axis=1, keepdims=True)
        bnorm[k] = jnp.broadcast_to(norm, (norm.shape[0], 128)).T[0:1]

    def tile(k, d):
        vv = (v + d) % 4
        gram = lax.dot_general(acat[vv], bbuf[u2(k)], NT, preferred_element_type=F32)
        tbuf[vv, k] = pack(bnorm[k] + anorm[vv, :, :40] - 2.0 * gram)
        pl.when(vv != y)(r1_out(vv, k).start)

    def tiles(first, last, ds):
        def one(k, carry):
            for d in ds:
                tile(k, d)
            return carry

        lax.fori_loop(first, last, one, 0)

    def reduce_all(first, last):
        def one(k, carry):
            reduce_y(k)
            return carry

        lax.fori_loop(first, last, one, 0)

    three_steps = jnp.minimum(steps, 3)

    def reduce_if(d):
        pl.when((v + d) % 4 == y)(lambda: reduce_all(0, three_steps))

    pl.semaphore_wait(down_sem.at[1], 1)
    signal(down_sem.at[2], below)
    relay_b(2)
    take_a(0)
    for k in range(3):
        pl.when(k < steps)(functools.partial(norm_of, k))
    tiles(0, three_steps, (0,))
    take_a(1)
    tiles(0, three_steps, (1,))
    pl.semaphore_wait(down_sem.at[2], 1)
    reduce_if(0)
    take_a(3)
    tiles(0, three_steps, (3,))
    reduce_if(1)
    take_a(2)
    tiles(0, three_steps, (2,))
    reduce_if(3)
    pl.semaphore_wait(plane_sem, 7)
    pl.semaphore_wait(near_sem, 15)

    @pl.when(steps == 4)
    def _():
        b_in(3).wait_recv()
        norm_of(3)
        tiles(3, 4, (0, 1, 3, 2))

    reduce_if(2)
    pl.when(steps == 4)(lambda: reduce_all(3, 4))

    def sw_out(k):
        return copy(swsend.at[k], swbuf.at[y // 2], sw_ss.at[k], sw_rs.at[y // 2], swap_to(k))

    def ow_out(k, xx):
        return copy(owsend.at[k, xx], owbuf.at[v // 2, x], ow_ss.at[k, xx], ow_rs.at[v // 2, x], own_to(k, xx))

    def swaps(k):
        return jnp.logical_or(c == 0, k > 0)

    def owns(k):
        return jnp.logical_or(c == 1, k > 0)

    def place(k, carry):
        copy(hsend.at[k], hbuf.at[k], h_ss.at[k], h_rs.at[k], other).wait_recv()
        packed = hsend[k] + hbuf[k]
        swsend[k] = packed
        same = is_me(swap_to(k))

        @pl.when(both(swaps(k), same))
        def _():
            swbuf[y // 2] = swsend[k]

        pl.when(both(swaps(k), no(same)))(sw_out(k).start)

        @pl.when(owns(k))
        def _():
            turned = unpack(packed)
            for xx in range(4):
                owsend[k, xx] = pack_quarter(turned[xx * 40 : xx * 40 + 40])
                same = is_me(own_to(k, xx))

                @pl.when(same)
                def _():
                    owbuf[v // 2, x] = owsend[k, xx]

                pl.when(no(same))(ow_out(k, xx).start)

        return carry

    lax.fori_loop(0, steps, place, 0)

    for b in range(2):

        @pl.when(no(is_me(swap_from[b])))
        def _():
            copy(swsend.at[0], swbuf.at[b], sw_ss.at[0], sw_rs.at[b], here).wait_recv()

        for xx in range(4):

            @pl.when(no(is_me(own_from[b][xx])))
            def _():
                copy(owsend.at[0, 0], owbuf.at[b, xx], ow_ss.at[0, 0], ow_rs.at[b, xx], here).wait_recv()

    values = []
    for b in range(2):
        own = jnp.concatenate([unpack_quarter(owbuf[b, xx]) for xx in range(4)], axis=1)
        values.append(jnp.exp(-(unpack(swbuf[b]).T + own) / scale))

    def d1_out(i):
        return copy(d1buf.at[4 * v + x], d1buf.at[4 * v + x], d1_ss, d1_rs, near_dev[i])

    for b in range(2):
        d1buf[4 * v + x, b] = jnp.sum(values[b], axis=0, keepdims=True)
    for i in range(15):
        d1_out(i).start()
    fifteen = d1buf.at[pl.ds(0, 15)]
    copy(fifteen, fifteen, d1_ss, d1_rs, here).wait_recv()
    density = d1buf[0]
    for i in range(1, 16):
        density = density + d1buf[i]

    def d2_out(i):
        return copy(d2buf.at[u], d2buf.at[u], d2_ss, d2_rs, ring_to[i])

    d2buf[u] = density
    for i in range(3):
        d2_out(i).start()
    three = d2buf.at[pl.ds(0, 3)]
    copy(three, three, d2_ss, d2_rs, here).wait_recv()
    density = d2buf[0] + d2buf[1] + d2buf[2] + d2buf[3]

    scaled = [values[b] / density[b] for b in range(2)]
    degree = jnp.sum(scaled[0], axis=1, keepdims=True) + jnp.sum(scaled[1], axis=1, keepdims=True)
    place = 2 * y + c

    def g_out(i):
        return copy(gbuf.at[place], gbuf.at[place], g_ss, g_rs, plane_dev[i])

    gbuf[place] = jnp.broadcast_to(degree, (40, 128)).T[0:1]
    for i in range(7):
        g_out(i).start()
    for d in range(1, 4):
        a_out(d).wait_send()
    for d in range(4):
        for e in range(1, 4):
            x_out(d, e).wait_send()
    for k in range(3):
        pl.when(both(passes, k < steps))(b_out(k).wait_send)

    def sent_tiles(k, carry):
        for vv in range(4):
            pl.when(vv != y)(r1_out(vv, k).wait_send)
        h_out(k).wait_send()
        return carry

    lax.fori_loop(0, steps, sent_tiles, 0)

    def sent_places(k, carry):
        pl.when(both(swaps(k), no(is_me(swap_to(k)))))(sw_out(k).wait_send)
        for xx in range(4):
            pl.when(both(owns(k), no(is_me(own_to(k, xx)))))(ow_out(k, xx).wait_send)
        return carry

    lax.fori_loop(0, steps, sent_places, 0)

    copy(fifteen, fifteen, d1_ss, d1_rs, here).wait_send()
    copy(three, three, d2_ss, d2_rs, here).wait_send()

    seven = gbuf.at[pl.ds(0, 7)]
    copy(seven, seven, g_ss, g_rs, here).wait_recv()
    degree = gbuf[0]
    for i in range(1, 8):
        degree = degree + gbuf[i]
    degree = jnp.broadcast_to(degree, (128, 40)).T[:, 0:1]
    o_ref[...] = total * jnp.where(h == 0, scaled[0], scaled[1]) / degree

    copy(seven, seven, g_ss, g_rs, here).wait_send()


def per_device(samples):
    rows, width = samples.shape
    total = 1.0 * rows * lax.axis_size("runs")
    scale = 4.0 * width * lax.axis_size("feat")
    dma = pltpu.SemaphoreType.DMA
    regular = pltpu.SemaphoreType.REGULAR
    vm = pltpu.VMEM
    return pl.pallas_call(
        functools.partial(kernel, total, scale),
        out_shape=jax.ShapeDtypeStruct((rows, 4 * rows), F32),
        in_specs=[pl.BlockSpec(memory_space=pl.ANY)],
        out_specs=pl.BlockSpec(memory_space=pltpu.VMEM),
        scratch_shapes=[
            vm((4, 4, rows, width), BF16),
            vm((4, rows, width), BF16),
            vm((4, 4 * rows, width), BF16),
            vm((4, 4 * rows, 128), F32),
            vm((4, 1, rows), F32),
            vm((4, 4, 56, 128), F32),
            vm((4, 4, 56, 128), F32),
            vm((4, 56, 128), F32),
            vm((4, 56, 128), F32),
            vm((4, 56, 128), F32),
            vm((4, 4, 16, 128), F32),
            vm((2, 56, 128), F32),
            vm((2, 4, 16, 128), F32),
            vm((16, 2, 1, 4 * rows), F32),
            vm((4, 2, 1, 4 * rows), F32),
            vm((8, 1, rows), F32),
            dma((4,)), dma((4,)),
            dma((4, 4)), dma((4, 4)),
            dma((3,)), dma((4,)),
            dma((4, 4)), dma((4, 4)),
            dma((4,)), dma((4,)),
            dma((4,)), dma((2,)),
            dma((4, 4)), dma((2, 4)),
            dma, dma,
            dma, dma,
            dma, dma,
            regular, regular((3,)), regular, regular, regular, dma,
        ],
        compiler_params=pltpu.CompilerParams(
            collective_id=0, has_side_effects=True, vmem_limit_bytes=48 << 20
        ),
        name="markov",
    )(pltpu.with_memory_space_constraint(samples, pltpu.HBM))


def solution(mesh):
    placed = P("runs", "feat")
    return jax.shard_map(per_device, mesh=mesh, in_specs=(placed,), out_specs=placed, check_vma=False)
```
